32 devices in a mesh: groups: 1, along: 8 (over z, y), across: 4 (over x, core).
Axes of the slice: x: 2, y: 2, z: 4, core: 2. Of those that a mesh axis runs over, the one named last changes fastest.
Arguments:
- doses: float32 [8, 4, 512], P(('groups', 'along'), 'across'), may hold values from 0.1 to 10
- shot_type: int32 [8, 4, 512], P(('groups', 'along'), 'across'), may hold values from 0 to 7
- shot_count: int32 [8, 4], P(('groups', 'along'), 'across'), may hold values from 1 to 512, as said below
- dose_weights: bfloat16 [8, 2048, 512], P(None, ('groups', 'along'), 'across'), may hold values from 0.019897461 to 1
- cotangent: float32 [2048, 512], P(('groups', 'along'), 'across'), may hold values from -6 to 6
Outputs:
- exposure: float32 [2048, 512], P(('groups', 'along'), 'across')
- dose_grad: float32 [8, 4, 512], P(('groups', 'along'), 'across')
The draws below stay inside these ranges and needn't reach their ends.
Inputs may be any that keep to these rules, and one draw needn't show every extreme that they name: Shot slots 0 to shot_count - 1 of a tile are live; some tile has all 512 live, some tile only one.
All inputs are finite; a program needn't handle non-finite values.
Results may differ from the reference program's by a relative error of at most 0.0003.
Values sent between devices are 32-bit elements; how exact they have to be, the bound alone decides.
A program may use at most 64 MiB of HBM per device.

```python
import math
import jax
import jax.numpy as jnp
from jax import lax

FA = 256
FC = 128
S = 512
K = 8
H = 16
TILES_A = 8
TILES_C = 4
NA = 2048
NC = 512


def draw_shot_count(key, part):
    key = jax.random.fold_in(key, 11)
    first_key, second_key = jax.random.split(key)
    number = TILES_A * TILES_C
    counts = jax.random.randint(first_key, (number,), 1, S + 1)
    place = jax.random.randint(second_key, (), 0, number)
    spots = jnp.arange(number)
    counts = jnp.where(spots == place, S, counts)
    counts = jnp.where(spots == (place + 1) % number, 1, counts)
    return counts.reshape(TILES_A, TILES_C).astype(jnp.int32)


def plant(entries, stream_key, smallest, high):
    spot = [jax.random.randint(jax.random.fold_in(stream_key, axis), (), 0, length) for axis, length in enumerate(entries.shape)]
    longest = entries.shape.index(max(entries.shape))
    beside = spot[:longest] + [(spot[longest] + 1) % entries.shape[longest]] + spot[longest + 1:]
    return entries.at[tuple(spot)].set(smallest).at[tuple(beside)].set(high)


def block_scale(stream_key, shape, shards, smallest, high):
    loudness, own = 1.0, jax.random.fold_in(stream_key, 6)
    for axis_at, parts in shards:
        draws = jnp.exp(jax.random.uniform(jax.random.fold_in(own, axis_at), (parts,), jnp.float32, smallest / len(shards), high / len(shards)))
        loudness = loudness * jnp.repeat(draws, shape[axis_at] // parts).reshape([-1 if axis == axis_at else 1 for axis in range(len(shape))])
    return loudness


def centred(rng, extent, scale, bound, cuts=(), held_as=jnp.bfloat16):
    drawn = jax.random.normal(rng, extent, jnp.float32) * scale
    if len(cuts) > 0:
        drawn = block_scale(rng, extent, cuts, -0.22, 0.18) * drawn
    return jnp.clip(drawn, min=-bound, max=bound).astype(held_as)


def setup_inputs(seed: int = 0, part: int = 0) -> dict:
    keys = jax.random.split(jax.random.key(seed), 6)
    part_splits = jax.random.split(jax.random.fold_in(keys[5], part), 6)
    return {
        "doses": jnp.clip(jnp.exp(math.log(10.0) - 4.6051702 * jax.random.uniform(part_splits[0], (TILES_A, TILES_C, S), jnp.float32) ** block_scale(part_splits[0], (TILES_A, TILES_C, S), ((0, 8), (1, 4)), -0.2, 0.2)), 0.1, 10.0),
        "shot_type": plant(jax.random.randint(part_splits[1], (TILES_A, TILES_C, S), 0, K), jax.random.fold_in(part_splits[1], 1), 0, K - 1).astype(jnp.int32),
        "shot_count": draw_shot_count(jax.random.fold_in(jax.random.fold_in(keys[5], part), 71), part),
        "dose_weights": jnp.clip(jnp.exp(math.log(1.0) - 3.9171631 * jax.random.uniform(part_splits[3], (K, NA, NC), jnp.float32) ** block_scale(part_splits[3], (K, NA, NC), ((1, 8), (2, 4)), -0.2, 0.2)), 0.019897461, 1.0).astype(jnp.bfloat16),
        "cotangent": centred(part_splits[4], (NA, NC), 1.0, 6.0, ((0, 8), (1, 4)), jnp.float32),
    }


sigma_fine = 3.75
sigma_back = 156.25
back_ratio = 0.7
exact = lax.Precision.HIGHEST

def fine_taps():
    reach = jnp.arange(-H, H + 1).astype(jnp.float32)
    weights = jnp.exp(-reach * reach / (2.0 * sigma_fine * sigma_fine))
    return weights / jnp.sum(weights)

def blur_fine(field):
    taps = fine_taps()
    padded = jnp.pad(field, ((H, H), (0, 0)))
    row_blur = taps[0] * padded[0:NA]
    for offset in range(1, 2 * H + 1):
        row_blur = row_blur + taps[offset] * padded[offset:offset + NA]
    padded = jnp.pad(row_blur, ((0, 0), (H, H)))
    result = taps[0] * padded[:, 0:NC]
    for offset in range(1, 2 * H + 1):
        result = result + taps[offset] * padded[:, offset:offset + NC]
    return result

def back_matrix(length):
    place = jnp.arange(length).astype(jnp.float32)
    distance = place[:, None] - place[None, :]
    return jnp.exp(-distance * distance / (2.0 * sigma_back * sigma_back)) / (math.sqrt(2.0 * math.pi) * sigma_back)

def blur_back(field):
    coarse = field.reshape(NA // 8, 8, NC // 8, 8).mean(axis=(1, 3))
    coarse = jnp.dot(back_matrix(NA // 8), coarse, precision=exact)
    coarse = jnp.dot(coarse, back_matrix(NC // 8), precision=exact)
    return jnp.repeat(jnp.repeat(coarse, 8, axis=0), 8, axis=1)

def operator_apply(field):
    return blur_fine(field) + back_ratio * blur_back(field)

def tile_sums(field):
    return field.reshape(NA // FA, FA, NC // FC, FC).sum(axis=(1, 3))

def dose_map(coef, dose_weights):
    total = jnp.zeros((NA, NC), jnp.float32)
    for kind in range(K):
        spread = jnp.repeat(jnp.repeat(coef[:, :, kind], FA, axis=0), FC, axis=1)
        total = total + spread * dose_weights[kind].astype(jnp.float32)
    return total

def forward(doses, shot_type, shot_count, dose_weights):
    shots = doses.shape[2]
    live = (jnp.arange(shots)[None, None, :] < shot_count[:, :, None]).astype(jnp.float32)
    onehot = (shot_type[:, :, :, None] == jnp.arange(K)[None, None, None, :]).astype(jnp.float32)
    coef = K / shots * lax.optimization_barrier(jnp.sum(onehot * (live * doses)[:, :, :, None], axis=2))
    totals = jnp.stack([tile_sums(dose_weights[kind].astype(jnp.float32)) for kind in range(K)], axis=2)
    for section in range(2):
        field = operator_apply(dose_map(coef, dose_weights))
        ratio = jnp.stack([tile_sums(dose_weights[kind].astype(jnp.float32) * field) for kind in range(K)], axis=2) / totals
        coef = coef / ratio
    return operator_apply(dose_map(coef, dose_weights))

def reference(doses, shot_type, shot_count, dose_weights, cotangent):
    final_field, pullback = jax.vjp(lambda given: forward(given, shot_type, shot_count, dose_weights), doses)
    grads = pullback(cotangent)
    return (final_field, grads[0])
```

```python
import functools
import math

import jax
import jax.numpy as jnp
import numpy as np
from jax import lax
from jax.experimental import pallas as pl
from jax.experimental.pallas import tpu as pltpu
from jax.sharding import PartitionSpec as P

H = 16
LANES = 128
BLOCK = 8
sigma_fine = 3.75
sigma_back = 156.25
back_ratio = 0.7
FIELDS = (2, 1, 2, 1)
reach = np.arange(-H, H + 1).astype(np.float64)
fine_norm = float(np.sum(np.exp(-reach * reach / (2.0 * sigma_fine * sigma_fine))))


def fine_weight(distance):
    d = distance.astype(jnp.float32)
    return jnp.where(
        jnp.abs(distance) <= H, jnp.exp(-d * d / (2.0 * sigma_fine * sigma_fine)) / fine_norm, 0.0
    )


def back_weight(distance, factor=1.0):
    d = distance.astype(jnp.float32)
    return jnp.exp(-d * d / (2.0 * sigma_back * sigma_back)) * (
        factor / (math.sqrt(2.0 * math.pi) * sigma_back)
    )


def iota(shape, dim):
    return lax.broadcasted_iota(jnp.int32, shape, dim)


def halves(value):
    high = value.astype(jnp.bfloat16)
    return high, (value - high.astype(jnp.float32)).astype(jnp.bfloat16)


def mm(a, b):
    return jnp.dot(a, b, preferred_element_type=jnp.float32)


def dot3(a, b):
    return mm(a[0], b[0]) + (mm(a[0], b[1]) + mm(a[1], b[0]))


def kernel(na, nc, *refs):
    doses_ref, type_ref, count_ref, w_ref, cot_ref, out_ref, grad_ref = refs[:7]
    (
        wf, fld, cols_h, cols_l, side_h, side_l, rows_h, rows_l, edge_h, edge_l,
        along_h, along_l, across_h, across_l,
    ) = refs[7:21]
    rounds = [refs[21 + 8 * t : 29 + 8 * t] for t in range(4)]
    local_sems, send_sems, recv_sems = refs[53:56]
    kinds, row_count, col_count = w_ref.shape
    coarse_rows = row_count // BLOCK
    coarse_cols = col_count // BLOCK
    groups = LANES // coarse_cols
    packed = coarse_rows // groups
    ia = lax.axis_index("along")
    ic = lax.axis_index("across")
    up, down = lax.rem(ia + na - 1, na), lax.rem(ia + 1, na)
    left, right = lax.rem(ic + nc - 1, nc), lax.rem(ic + 1, nc)
    along_peers = [lax.rem(ia + o, na) for o in range(1, na)]
    across_peers = [lax.rem(ic + o, nc) for o in range(1, nc)]

    barrier = pltpu.get_barrier_semaphore()
    greeted = (
        [{"along": a} for a in along_peers]
        + [{"across": c} for c in across_peers]
        + [{"along": a, "across": c} for a in (up, down) for c in (left, right)]
    )
    for device in greeted:
        pl.semaphore_signal(barrier, inc=1, device_id=device, device_id_type=pl.DeviceIdType.MESH)

    lane_group = iota((groups, LANES), 1) // coarse_cols
    own_group = lane_group == iota((groups, LANES), 0)
    pool = jnp.where(
        iota((col_count, LANES), 0) // BLOCK == iota((col_count, LANES), 1) % coarse_cols,
        1.0 / (BLOCK * BLOCK),
        0.0,
    ).astype(jnp.bfloat16)
    repeat = jnp.where(
        iota((LANES, LANES), 0) % coarse_cols == iota((LANES, LANES), 1) % coarse_cols, 1.0, 0.0
    ).astype(jnp.bfloat16)

    def dose_map(coef):
        total = coef[0:1] * wf[0]
        for kind in range(1, kinds):
            total = total + coef[kind : kind + 1] * wf[kind]
        return total

    def weighted(field):
        sums = []
        for kind in range(kinds):
            value = wf[kind] if field is None else wf[kind] * field
            part = value.reshape(row_count // 8, 8, col_count).sum(axis=0)
            sums.append(jnp.sum(part, axis=0, keepdims=True))
        return jnp.broadcast_to(
            jnp.sum(jnp.concatenate(sums, axis=0), axis=1, keepdims=True), (kinds, col_count)
        )

    def remote(src, dst, t, which, device):
        pltpu.make_async_remote_copy(
            src_ref=src,
            dst_ref=dst,
            send_sem=send_sems.at[t, which],
            recv_sem=recv_sems.at[t, which],
            device_id=device,
            device_id_type=pl.DeviceIdType.MESH,
        ).start()

    def wait_for(ref, sem):
        pltpu.make_async_copy(ref, ref, sem).wait()

    def send_first(t, fields):
        ca, cb, strip, side, ga, gb, halo_rows, halo_cols = rounds[t]
        for f, field in enumerate(fields):
            high, low = halves(field)
            pooled = mm(high, pool) + mm(low, pool)
            for r in range(packed):
                total = None
                for g in range(groups):
                    start = (r * groups + g) * BLOCK
                    term = jnp.where(lane_group == g, pooled[start : start + BLOCK], 0.0)
                    total = term if total is None else total + term
                ca[packed * f + r : packed * f + r + 1] = jnp.sum(total, axis=0, keepdims=True)
        pltpu.make_async_copy(ca, ga.at[ia], recv_sems.at[t, 0]).start()
        for peer in along_peers:
            remote(ca, ga.at[ia], t, 0, {"along": peer})
        for f, field in enumerate(fields):
            strip[0, f] = field[:H]
            strip[1, f] = field[row_count - H :]
            fld[f] = field
        for slot, c in ((1, None), (2, left), (0, right)):
            for tb, a in ((0, up), (1, down)):
                device = {"along": a} if c is None else {"along": a, "across": c}
                remote(strip.at[tb], halo_rows.at[slot, 1 - tb], t, 1, device)
        for f, field in enumerate(fields):
            turned = field.T
            side[0, f] = turned[:H]
            side[1, f] = turned[col_count - H :]
        remote(side.at[0], halo_cols.at[1], t, 2, {"across": left})
        remote(side.at[1], halo_cols.at[0], t, 2, {"across": right})

    def spread(row):
        return jnp.where(own_group, jnp.broadcast_to(row, (groups, LANES)), 0.0)

    def finish(t):
        ca, cb, strip, side, ga, gb, halo_rows, halo_cols = rounds[t]
        count = FIELDS[t]
        wait_for(ga, recv_sems.at[t, 0])
        theirs = jnp.concatenate(
            [
                jnp.concatenate(
                    [
                        spread(ga[a, packed * f + r : packed * f + r + 1])
                        for a in range(na)
                        for r in range(packed)
                    ],
                    axis=0,
                )
                for f in range(count)
            ],
            axis=1,
        )
        blurred = dot3((along_h[...], along_l[...]), halves(theirs))
        blurred = jnp.concatenate(
            [blurred[:, f * LANES : (f + 1) * LANES] for f in range(count)], axis=0
        )
        high, low = halves(blurred)
        blurred = mm(high, repeat) + mm(low, repeat)
        for i in range(packed * count):
            part = jnp.where(own_group, blurred[i * groups : (i + 1) * groups], 0.0)
            cb[i : i + 1] = jnp.sum(part, axis=0, keepdims=True)
        pltpu.make_async_copy(cb, gb.at[ic], recv_sems.at[t, 3]).start()
        for peer in across_peers:
            remote(cb, gb.at[ic], t, 3, {"across": peer})

        wait_for(halo_rows, recv_sems.at[t, 1])
        wait_for(halo_cols, recv_sems.at[t, 2])
        middles, edges = [], []
        cols = (cols_h[...], cols_l[...])
        centre = (cols_h[col_count : 2 * col_count], cols_l[col_count : 2 * col_count])
        for f in range(count):
            beside = jnp.concatenate([halo_cols[0, f], halo_cols[1, f]], axis=0).T
            middles.append(
                dot3(halves(fld[f]), centre) + dot3(halves(beside), (side_h[...], side_l[...]))
            )
            outer = jnp.concatenate(
                [
                    jnp.concatenate([halo_rows[s, 0, f], halo_rows[s, 1, f]], axis=0)
                    for s in range(3)
                ],
                axis=1,
            )
            edges.append(dot3(halves(outer), cols))
        middle = jnp.concatenate(middles, axis=1)
        edge = jnp.concatenate(edges, axis=1)
        fine = dot3((rows_h[...], rows_l[...]), halves(middle)) + dot3(
            (edge_h[...], edge_l[...]), halves(edge)
        )

        wait_for(gb, recv_sems.at[t, 3])
        both = jnp.concatenate(
            [
                jnp.concatenate([spread(gb[c, i : i + 1]) for c in range(nc)], axis=1)
                for i in range(packed * count)
            ],
            axis=0,
        )
        back = dot3(halves(both), (across_h[...], across_l[...]))
        results = []
        for f in range(count):
            wide = jnp.concatenate(
                [
                    jnp.broadcast_to(back[p : p + 1], (BLOCK, col_count))
                    for p in range(f * coarse_rows, (f + 1) * coarse_rows)
                ],
                axis=0,
            )
            results.append(fine[:, f * col_count : (f + 1) * col_count] + wide)
        return results

    shots = doses_ref.shape[-1]
    share = kinds / shots
    live = (iota((1, shots), 1) < count_ref[...]).astype(jnp.float32)
    chosen = (type_ref[0] == iota((kinds, shots), 0)).astype(jnp.float32)
    coef0 = share * jnp.broadcast_to(
        jnp.sum(chosen * (live * doses_ref[0]), axis=1, keepdims=True), (kinds, col_count)
    )
    for kind in range(kinds):
        wf[kind] = w_ref[kind].astype(jnp.float32)
    first = dose_map(coef0)

    pl.semaphore_wait(barrier, len(greeted))
    send_first(0, [first, cot_ref[...]])

    def keep(refs_pair, value):
        refs_pair[0][...], refs_pair[1][...] = halves(value)

    shape = (coarse_rows, na * coarse_rows)
    keep((along_h, along_l), back_weight(ia * coarse_rows + iota(shape, 0) - iota(shape, 1)))
    shape = (col_count, col_count)
    gap = iota(shape, 1) - iota(shape, 0)
    lefts = jnp.where(ic > 0, fine_weight(gap + col_count), 0.0)
    rights = jnp.where(ic < nc - 1, fine_weight(gap - col_count), 0.0)
    keep((cols_h, cols_l), jnp.concatenate([lefts, fine_weight(gap), rights], axis=0))
    keep((side_h, side_l), jnp.concatenate([lefts[col_count - H :], rights[:H]], axis=0))
    shape = (row_count, row_count)
    keep((rows_h, rows_l), fine_weight(iota(shape, 0) - iota(shape, 1)))
    shape = (row_count, 2 * H)
    spot = iota(shape, 1)
    above = jnp.where(ia > 0, fine_weight(iota(shape, 0) - (spot - H)), 0.0)
    below = jnp.where(ia < na - 1, fine_weight(iota(shape, 0) - (spot - H + row_count)), 0.0)
    keep((edge_h, edge_l), jnp.where(spot < H, above, below))
    shape = (nc * LANES, col_count)
    source = iota(shape, 0) // LANES * coarse_cols + iota(shape, 0) % coarse_cols
    keep(
        (across_h, across_l),
        back_weight(source - (ic * coarse_cols + iota(shape, 1) // BLOCK), back_ratio),
    )
    totals = weighted(None)

    field, pulled = finish(0)
    ratio0 = weighted(field) / totals
    coef1 = coef0 / ratio0
    send_first(1, [dose_map(coef1)])
    grad2 = weighted(pulled)

    (field,) = finish(1)
    ratio1 = weighted(field) / totals
    coef2 = coef1 / ratio1
    grad_ratio1 = -grad2 * coef2 / ratio1
    send_first(2, [dose_map(coef2), dose_map(grad_ratio1 / totals)])

    exposure, field = finish(2)
    grad1 = grad2 / ratio1 + weighted(field)
    grad_ratio0 = -grad1 * coef1 / ratio0
    send_first(3, [dose_map(grad_ratio0 / totals)])
    out_ref[...] = exposure

    (field,) = finish(3)
    grad0 = grad1 / ratio0 + weighted(field)
    grad_ref[0] = live * share * jnp.sum(chosen * grad0[:, 0:1], axis=0, keepdims=True)

    for t in range(4):
        ca, cb, strip, side, ga, gb, halo_rows, halo_cols = rounds[t]
        wait_for(ga.at[: na - 1], send_sems.at[t, 0])
        wait_for(halo_rows, send_sems.at[t, 1])
        wait_for(halo_cols, send_sems.at[t, 2])
        wait_for(gb.at[: nc - 1], send_sems.at[t, 3])


def shards(na, nc, doses, shot_type, shot_count, dose_weights, cotangent):
    kinds, rows, cols = dose_weights.shape
    f32, bf16 = jnp.float32, jnp.bfloat16
    coarse_rows = rows // BLOCK
    packed = coarse_rows * (cols // BLOCK) // LANES

    def pair(*shape):
        return [pltpu.VMEM(shape, bf16), pltpu.VMEM(shape, bf16)]

    scratch = [pltpu.VMEM((kinds, rows, cols), f32), pltpu.VMEM((2, rows, cols), f32)]
    scratch += pair(3 * cols, cols) + pair(2 * H, cols) + pair(rows, rows) + pair(rows, 2 * H)
    scratch += pair(coarse_rows, na * coarse_rows) + pair(nc * LANES, cols)
    for count in FIELDS:
        scratch += [
            pltpu.VMEM((packed * count, LANES), f32),
            pltpu.VMEM((packed * count, LANES), f32),
            pltpu.VMEM((2, count, H, cols), f32),
            pltpu.VMEM((2, count, H, rows), f32),
            pltpu.VMEM((na, packed * count, LANES), f32),
            pltpu.VMEM((nc, packed * count, LANES), f32),
            pltpu.VMEM((3, 2, count, H, cols), f32),
            pltpu.VMEM((2, count, H, rows), f32),
        ]
    scratch += [
        pltpu.SemaphoreType.DMA((4,)),
        pltpu.SemaphoreType.DMA((4, 4)),
        pltpu.SemaphoreType.DMA((4, 4)),
    ]
    return pl.pallas_call(
        functools.partial(kernel, na, nc),
        out_shape=(
            jax.ShapeDtypeStruct(cotangent.shape, f32),
            jax.ShapeDtypeStruct(doses.shape, f32),
        ),
        in_specs=[pl.BlockSpec(memory_space=pltpu.VMEM)] * 5,
        out_specs=(pl.BlockSpec(memory_space=pltpu.VMEM),) * 2,
        scratch_shapes=scratch,
        compiler_params=pltpu.CompilerParams(
            collective_id=0, has_side_effects=True, vmem_limit_bytes=32 * 1024 * 1024
        ),
    )(doses, shot_type, shot_count, dose_weights, cotangent)


def solution(mesh):
    in_specs = (
        P(("groups", "along"), "across", None),
        P(("groups", "along"), "across", None),
        P(("groups", "along"), "across"),
        P(None, ("groups", "along"), "across"),
        P(("groups", "along"), "across"),
    )
    out_specs = (P(("groups", "along"), "across"), P(("groups", "along"), "across", None))
    run = functools.partial(shards, mesh.shape["along"], mesh.shape["across"])
    return jax.shard_map(run, mesh=mesh, in_specs=in_specs, out_specs=out_specs, check_vma=False)
```

```python
import functools
import math

import jax
import jax.numpy as jnp
import numpy as np
from jax import lax
from jax.experimental import pallas as pl
from jax.experimental.pallas import tpu as pltpu
from jax.sharding import PartitionSpec as P

H = 16
LANES = 128
BLOCK = 8
sigma_fine = 3.75
sigma_back = 156.25
back_ratio = 0.7
JOBS = 6
COTANGENT, EXPOSURE = 4, 5
reach = np.arange(-H, H + 1).astype(np.float64)
fine_norm = float(np.sum(np.exp(-reach * reach / (2.0 * sigma_fine * sigma_fine))))


def fine_weight(distance):
    d = distance.astype(jnp.float32)
    return jnp.where(
        jnp.abs(distance) <= H, jnp.exp(-d * d / (2.0 * sigma_fine * sigma_fine)) / fine_norm, 0.0
    )


def back_weight(distance, factor=1.0):
    d = distance.astype(jnp.float32)
    return jnp.exp(-d * d / (2.0 * sigma_back * sigma_back)) * (
        factor / (math.sqrt(2.0 * math.pi) * sigma_back)
    )


def iota(shape, dim):
    return lax.broadcasted_iota(jnp.int32, shape, dim)


def halves(value):
    high = value.astype(jnp.bfloat16)
    return high, (value - high.astype(jnp.float32)).astype(jnp.bfloat16)


def mm(a, b):
    return jnp.dot(a, b, preferred_element_type=jnp.float32)


def dot3(a, b):
    return mm(a[0], b[0]) + (mm(a[0], b[1]) + mm(a[1], b[0]))


def kernel(na, nc, *refs):
    doses_ref, type_ref, count_ref, w_ref, cot_ref, out_ref, grad_ref = refs[:7]
    (
        wf, fld, fine, cols_h, cols_l, side3, rows_h, rows_l, edge3, along3, across_h, across_l,
    ) = refs[7:19]
    jobs = [refs[19 + 6 * t : 25 + 6 * t] for t in range(JOBS)]
    send_sems, recv_sems = refs[19 + 6 * JOBS :]
    kinds, row_count, col_count = w_ref.shape
    coarse_rows = row_count // BLOCK
    coarse_cols = col_count // BLOCK
    groups = LANES // coarse_cols
    packed = coarse_rows // groups
    ia = lax.axis_index("along")
    ic = lax.axis_index("across")
    along_at = [lax.rem(ia + o, na) for o in range(na)]
    across_at = [lax.rem(ic + o, nc) for o in range(nc)]
    up, down = along_at[na - 1], along_at[1]
    left, right = across_at[nc - 1], across_at[1]
    offsets = sorted(range(na), key=lambda o: -min(o, na - o))
    peers = [
        {"along": along_at[oa], "across": across_at[oc]}
        for oa in offsets
        for oc in range(nc)
        if oa or oc
    ]

    barrier = pltpu.get_barrier_semaphore()
    for device in peers:
        pl.semaphore_signal(barrier, inc=1, device_id=device, device_id_type=pl.DeviceIdType.MESH)

    lane_group = iota((groups, LANES), 1) // coarse_cols
    pool = jnp.where(
        iota((col_count, LANES), 0) // BLOCK == iota((col_count, LANES), 1) % coarse_cols,
        1.0 / (BLOCK * BLOCK),
        0.0,
    ).astype(jnp.bfloat16)

    def dose_map(coef):
        total = coef[0:1] * wf[0]
        for kind in range(1, kinds):
            total = total + coef[kind : kind + 1] * wf[kind]
        return total

    def weighted(field):
        sums = []
        for kind in range(kinds):
            value = wf[kind] if field is None else wf[kind] * field
            part = value.reshape(row_count // 8, 8, col_count).sum(axis=0)
            sums.append(jnp.sum(part, axis=0, keepdims=True))
        return jnp.broadcast_to(
            jnp.sum(jnp.concatenate(sums, axis=0), axis=1, keepdims=True), (kinds, col_count)
        )

    def remote(src, dst, t, which, device):
        pltpu.make_async_remote_copy(
            src_ref=src,
            dst_ref=dst,
            send_sem=send_sems.at[t, which],
            recv_sem=recv_sems.at[t, which],
            device_id=device,
            device_id_type=pl.DeviceIdType.MESH,
        ).start()

    def wait_for(ref, sem):
        pltpu.make_async_copy(ref, ref, sem).wait()

    mine = ia * nc + ic

    def send(t, field):
        ca, strip, side, ga, halo_rows, halo_cols = jobs[t]
        high, low = halves(field)
        pooled = mm(high, pool) + mm(low, pool)
        for r in range(packed):
            total = None
            for g in range(groups):
                start = (r * groups + g) * BLOCK
                term = jnp.where(lane_group == g, pooled[start : start + BLOCK], 0.0)
                total = term if total is None else total + term
            ca[r : r + 1] = jnp.sum(total, axis=0, keepdims=True)
        for device in peers:
            remote(ca, ga.at[mine], t, 0, device)
        pltpu.make_async_copy(ca, ga.at[mine], recv_sems.at[t, 0]).start()
        strip[0] = field[:H]
        strip[1] = field[row_count - H :]
        turned = field.T
        side[0] = turned[:H]
        side[1] = turned[col_count - H :]
        for slot, c in ((1, ic), (2, left), (0, right)):
            for tb, a in ((0, up), (1, down)):
                device = {"along": a, "across": c}
                remote(strip.at[tb], halo_rows.at[slot, 1 - tb], t, 1, device)
        remote(side.at[0], halo_cols.at[1], t, 2, {"along": ia, "across": left})
        remote(side.at[1], halo_cols.at[0], t, 2, {"along": ia, "across": right})
        fld[t] = field

    def inside(t):
        centre = (cols_h[col_count : 2 * col_count], cols_l[col_count : 2 * col_count])
        middle = dot3(halves(fld[t]), centre)
        fine[t] = dot3((rows_h[...], rows_l[...]), halves(middle))

    def finish(t):
        ca, strip, side, ga, halo_rows, halo_cols = jobs[t]
        wait_for(halo_rows, recv_sems.at[t, 1])
        wait_for(halo_cols, recv_sems.at[t, 2])
        high, low = halves(jnp.concatenate([halo_cols[0], halo_cols[1]], axis=0).T)
        beside = mm(jnp.concatenate([high, low, high], axis=1), side3[...])
        outer = jnp.concatenate(
            [jnp.concatenate([halo_rows[s, 0], halo_rows[s, 1]], axis=0) for s in range(3)], axis=1
        )
        high, low = halves(dot3(halves(outer), (cols_h[...], cols_l[...])))
        edges = mm(edge3[...], jnp.concatenate([high, low, high], axis=0))
        result = fine[t] + (dot3((rows_h[...], rows_l[...]), halves(beside)) + edges)

        wait_for(ga, recv_sems.at[t, 0])
        theirs = jnp.concatenate(
            [
                jnp.concatenate([ga[a * nc + c] for a in range(na)], axis=0)
                for c in range(nc)
            ],
            axis=1,
        )
        high, low = halves(theirs)
        every = mm(along3[...], jnp.concatenate([high, low, high], axis=0))
        picked = None
        group = iota((coarse_rows, nc * LANES), 1) % LANES // coarse_cols
        for g in range(groups):
            term = jnp.where(group == g, every[g * coarse_rows : (g + 1) * coarse_rows], 0.0)
            picked = term if picked is None else picked + term
        back = dot3(halves(picked), (across_h[...], across_l[...]))
        return result + jnp.concatenate(
            [jnp.broadcast_to(back[p : p + 1], (BLOCK, col_count)) for p in range(coarse_rows)],
            axis=0,
        )

    shots = doses_ref.shape[-1]
    share = kinds / shots
    live = (iota((1, shots), 1) < count_ref[...]).astype(jnp.float32)
    chosen = (type_ref[0] == iota((kinds, shots), 0)).astype(jnp.float32)
    coef0 = share * jnp.broadcast_to(
        jnp.sum(chosen * (live * doses_ref[0]), axis=1, keepdims=True), (kinds, col_count)
    )
    for kind in range(kinds):
        wf[kind] = w_ref[kind].astype(jnp.float32)
    first = dose_map(coef0)

    pl.semaphore_wait(barrier, len(peers))
    send(0, first)
    send(COTANGENT, cot_ref[...])

    shape = (col_count, col_count)
    gap = iota(shape, 1) - iota(shape, 0)
    lefts = jnp.where(ic > 0, fine_weight(gap + col_count), 0.0)
    rights = jnp.where(ic < nc - 1, fine_weight(gap - col_count), 0.0)
    cols_h[...], cols_l[...] = halves(jnp.concatenate([lefts, fine_weight(gap), rights], axis=0))
    high, low = halves(jnp.concatenate([lefts[col_count - H :], rights[:H]], axis=0))
    side3[...] = jnp.concatenate([high, high, low], axis=0)
    shape = (row_count, row_count)
    rows_h[...], rows_l[...] = halves(fine_weight(iota(shape, 0) - iota(shape, 1)))
    shape = (row_count, 2 * H)
    spot = iota(shape, 1)
    above = jnp.where(ia > 0, fine_weight(iota(shape, 0) - (spot - H)), 0.0)
    below = jnp.where(ia < na - 1, fine_weight(iota(shape, 0) - (spot - H + row_count)), 0.0)
    high, low = halves(jnp.where(spot < H, above, below))
    edge3[...] = jnp.concatenate([high, high, low], axis=1)
    shape = (groups * coarse_rows, na * packed)
    target = ia * coarse_rows + iota(shape, 0) % coarse_rows
    high, low = halves(back_weight(target - (iota(shape, 1) * groups + iota(shape, 0) // coarse_rows)))
    along3[...] = jnp.concatenate([high, high, low], axis=1)
    shape = (nc * LANES, col_count)
    source = iota(shape, 0) // LANES * coarse_cols + iota(shape, 0) % coarse_cols
    across_h[...], across_l[...] = halves(
        back_weight(source - (ic * coarse_cols + iota(shape, 1) // BLOCK), back_ratio)
    )
    totals = weighted(None)

    inside(0)
    ratio0 = weighted(finish(0)) / totals
    coef1 = coef0 / ratio0
    send(1, dose_map(coef1))

    inside(1)
    inside(COTANGENT)
    grad2 = weighted(finish(COTANGENT))
    ratio1 = weighted(finish(1)) / totals
    coef2 = coef1 / ratio1
    grad_ratio1 = -grad2 * coef2 / ratio1
    send(2, dose_map(grad_ratio1 / totals))
    send(EXPOSURE, dose_map(coef2))

    inside(2)
    grad1 = grad2 / ratio1 + weighted(finish(2))
    grad_ratio0 = -grad1 * coef1 / ratio0
    send(3, dose_map(grad_ratio0 / totals))

    inside(3)
    inside(EXPOSURE)
    out_ref[...] = finish(EXPOSURE)
    grad0 = grad1 / ratio0 + weighted(finish(3))
    grad_ref[0] = live * share * jnp.sum(chosen * grad0[:, 0:1], axis=0, keepdims=True)

    for t in range(JOBS):
        ca, strip, side, ga, halo_rows, halo_cols = jobs[t]
        wait_for(ga.at[: na * nc - 1], send_sems.at[t, 0])
        wait_for(halo_rows, send_sems.at[t, 1])
        wait_for(halo_cols, send_sems.at[t, 2])


def shards(na, nc, doses, shot_type, shot_count, dose_weights, cotangent):
    kinds, rows, cols = dose_weights.shape
    f32, bf16 = jnp.float32, jnp.bfloat16
    coarse_rows = rows // BLOCK
    packed = coarse_rows * (cols // BLOCK) // LANES

    def pair(*shape):
        return [pltpu.VMEM(shape, bf16), pltpu.VMEM(shape, bf16)]

    scratch = [pltpu.VMEM((kinds, rows, cols), f32)] + [pltpu.VMEM((JOBS, rows, cols), f32)] * 2
    scratch += pair(3 * cols, cols) + [pltpu.VMEM((6 * H, cols), bf16)]
    scratch += pair(rows, rows) + [pltpu.VMEM((rows, 6 * H), bf16)]
    groups = coarse_rows // packed
    scratch += [pltpu.VMEM((groups * coarse_rows, 3 * na * packed), bf16)] + pair(nc * LANES, cols)
    for _ in range(JOBS):
        scratch += [
            pltpu.VMEM((packed, LANES), f32),
            pltpu.VMEM((2, H, cols), f32),
            pltpu.VMEM((2, H, rows), f32),
            pltpu.VMEM((na * nc, packed, LANES), f32),
            pltpu.VMEM((3, 2, H, cols), f32),
            pltpu.VMEM((2, H, rows), f32),
        ]
    scratch += [pltpu.SemaphoreType.DMA((JOBS, 3)), pltpu.SemaphoreType.DMA((JOBS, 3))]
    return pl.pallas_call(
        functools.partial(kernel, na, nc),
        out_shape=(
            jax.ShapeDtypeStruct(cotangent.shape, f32),
            jax.ShapeDtypeStruct(doses.shape, f32),
        ),
        in_specs=[pl.BlockSpec(memory_space=pltpu.VMEM)] * 5,
        out_specs=(pl.BlockSpec(memory_space=pltpu.VMEM),) * 2,
        scratch_shapes=scratch,
        compiler_params=pltpu.CompilerParams(
            collective_id=0, has_side_effects=True, vmem_limit_bytes=32 * 1024 * 1024
        ),
    )(doses, shot_type, shot_count, dose_weights, cotangent)


def solution(mesh):
    in_specs = (
        P(("groups", "along"), "across", None),
        P(("groups", "along"), "across", None),
        P(("groups", "along"), "across"),
        P(None, ("groups", "along"), "across"),
        P(("groups", "along"), "across"),
    )
    out_specs = (P(("groups", "along"), "across"), P(("groups", "along"), "across", None))
    run = functools.partial(shards, mesh.shape["along"], mesh.shape["across"])
    return jax.shard_map(run, mesh=mesh, in_specs=in_specs, out_specs=out_specs, check_vma=False)
```

```python
import functools
import math

import jax
import jax.numpy as jnp
import numpy as np
from jax import lax
from jax.experimental import pallas as pl
from jax.experimental.pallas import tpu as pltpu
from jax.sharding import PartitionSpec as P

H = 16
LANES = 128
BLOCK = 8
sigma_fine = 3.75
sigma_back = 156.25
back_ratio = 0.7
JOBS = 6
COTANGENT, EXPOSURE = 4, 5
reach = np.arange(-H, H + 1).astype(np.float64)
fine_norm = float(np.sum(np.exp(-reach * reach / (2.0 * sigma_fine * sigma_fine))))


def fine_weight(distance):
    d = distance.astype(jnp.float32)
    return jnp.where(
        jnp.abs(distance) <= H, jnp.exp(-d * d / (2.0 * sigma_fine * sigma_fine)) / fine_norm, 0.0
    )


def back_weight(distance, factor=1.0):
    d = distance.astype(jnp.float32)
    return jnp.exp(-d * d / (2.0 * sigma_back * sigma_back)) * (
        factor / (math.sqrt(2.0 * math.pi) * sigma_back)
    )


def iota(shape, dim):
    return lax.broadcasted_iota(jnp.int32, shape, dim)


def halves(value):
    high = value.astype(jnp.bfloat16)
    return high, (value - high.astype(jnp.float32)).astype(jnp.bfloat16)


def mm(a, b):
    return jnp.dot(a, b, preferred_element_type=jnp.float32)


def dot3(a, b):
    return mm(a[0], b[0]) + (mm(a[0], b[1]) + mm(a[1], b[0]))


def kernel(na, nc, *refs):
    *sources, out_ref, grad_ref = refs[:7]
    (
        wf, fld, fine, cols_h, cols_l, side3, rows_h, rows_l, edge3, along3, across_h, across_l,
    ) = refs[7:19]
    jobs = [refs[19 + 6 * t : 25 + 6 * t] for t in range(JOBS)]
    send_sems, recv_sems, load_sems, *held = refs[19 + 6 * JOBS :]
    doses_ref, type_ref, count_ref, w_ref, cot_ref = held
    loads = [
        pltpu.make_async_copy(source, target, load_sems.at[n])
        for n, (source, target) in enumerate(zip(sources, held))
    ]
    for n in (3, 0, 1, 2, 4):
        loads[n].start()
    kinds, row_count, col_count = w_ref.shape
    coarse_rows = row_count // BLOCK
    coarse_cols = col_count // BLOCK
    groups = LANES // coarse_cols
    packed = coarse_rows // groups
    ia = lax.axis_index("along")
    ic = lax.axis_index("across")
    along_at = [lax.rem(ia + o, na) for o in range(na)]
    across_at = [lax.rem(ic + o, nc) for o in range(nc)]
    up, down = along_at[na - 1], along_at[1]
    left, right = across_at[nc - 1], across_at[1]
    offsets = sorted(range(na), key=lambda o: -min(o, na - o))
    peers = [
        {"along": along_at[oa], "across": across_at[oc]}
        for oa in offsets
        for oc in range(nc)
        if oa or oc
    ]

    barrier = pltpu.get_barrier_semaphore()
    for device in peers:
        pl.semaphore_signal(barrier, inc=1, device_id=device, device_id_type=pl.DeviceIdType.MESH)

    lane_group = iota((groups, LANES), 1) // coarse_cols
    pool = jnp.where(
        iota((col_count, LANES), 0) // BLOCK == iota((col_count, LANES), 1) % coarse_cols,
        1.0 / (BLOCK * BLOCK),
        0.0,
    ).astype(jnp.bfloat16)

    def dose_map(coef):
        total = coef[0:1] * wf[0]
        for kind in range(1, kinds):
            total = total + coef[kind : kind + 1] * wf[kind]
        return total

    def weighted(field):
        sums = []
        for kind in range(kinds):
            value = wf[kind] if field is None else wf[kind] * field
            part = value.reshape(row_count // 8, 8, col_count).sum(axis=0)
            sums.append(jnp.sum(part, axis=0, keepdims=True))
        return jnp.broadcast_to(
            jnp.sum(jnp.concatenate(sums, axis=0), axis=1, keepdims=True), (kinds, col_count)
        )

    def remote(src, dst, t, which, device):
        pltpu.make_async_remote_copy(
            src_ref=src,
            dst_ref=dst,
            send_sem=send_sems.at[t, which],
            recv_sem=recv_sems.at[t, which],
            device_id=device,
            device_id_type=pl.DeviceIdType.MESH,
        ).start()

    def wait_for(ref, sem):
        pltpu.make_async_copy(ref, ref, sem).wait()

    mine = ia * nc + ic

    def send(t, field):
        ca, strip, side, ga, halo_rows, halo_cols = jobs[t]
        high, low = halves(field)
        pooled = mm(high, pool) + mm(low, pool)
        for r in range(packed):
            total = None
            for g in range(groups):
                start = (r * groups + g) * BLOCK
                term = jnp.where(lane_group == g, pooled[start : start + BLOCK], 0.0)
                total = term if total is None else total + term
            ca[r : r + 1] = jnp.sum(total, axis=0, keepdims=True)
        for device in peers:
            remote(ca, ga.at[mine], t, 0, device)
        pltpu.make_async_copy(ca, ga.at[mine], recv_sems.at[t, 0]).start()
        strip[0] = field[:H]
        strip[1] = field[row_count - H :]
        turned = field.T
        side[0] = turned[:H]
        side[1] = turned[col_count - H :]
        for slot, c in ((1, ic), (2, left), (0, right)):
            for tb, a in ((0, up), (1, down)):
                device = {"along": a, "across": c}
                remote(strip.at[tb], halo_rows.at[slot, 1 - tb], t, 1, device)
        remote(side.at[0], halo_cols.at[1], t, 2, {"along": ia, "across": left})
        remote(side.at[1], halo_cols.at[0], t, 2, {"along": ia, "across": right})
        fld[t] = field

    def inside(t):
        centre = (cols_h[col_count : 2 * col_count], cols_l[col_count : 2 * col_count])
        middle = dot3(halves(fld[t]), centre)
        fine[t] = dot3((rows_h[...], rows_l[...]), halves(middle))

    def finish(t):
        ca, strip, side, ga, halo_rows, halo_cols = jobs[t]
        wait_for(halo_rows, recv_sems.at[t, 1])
        wait_for(halo_cols, recv_sems.at[t, 2])
        high, low = halves(jnp.concatenate([halo_cols[0], halo_cols[1]], axis=0).T)
        beside = mm(jnp.concatenate([high, low, high], axis=1), side3[...])
        outer = jnp.concatenate(
            [jnp.concatenate([halo_rows[s, 0], halo_rows[s, 1]], axis=0) for s in range(3)], axis=1
        )
        high, low = halves(dot3(halves(outer), (cols_h[...], cols_l[...])))
        edges = mm(edge3[...], jnp.concatenate([high, low, high], axis=0))
        result = fine[t] + (dot3((rows_h[...], rows_l[...]), halves(beside)) + edges)

        wait_for(ga, recv_sems.at[t, 0])
        theirs = jnp.concatenate(
            [
                jnp.concatenate([ga[a * nc + c] for a in range(na)], axis=0)
                for c in range(nc)
            ],
            axis=1,
        )
        high, low = halves(theirs)
        every = mm(along3[...], jnp.concatenate([high, low, high], axis=0))
        picked = None
        group = iota((coarse_rows, nc * LANES), 1) % LANES // coarse_cols
        for g in range(groups):
            term = jnp.where(group == g, every[g * coarse_rows : (g + 1) * coarse_rows], 0.0)
            picked = term if picked is None else picked + term
        back = dot3(halves(picked), (across_h[...], across_l[...]))
        return result + jnp.concatenate(
            [jnp.broadcast_to(back[p : p + 1], (BLOCK, col_count)) for p in range(coarse_rows)],
            axis=0,
        )

    shape = (col_count, col_count)
    gap = iota(shape, 1) - iota(shape, 0)
    lefts = jnp.where(ic > 0, fine_weight(gap + col_count), 0.0)
    rights = jnp.where(ic < nc - 1, fine_weight(gap - col_count), 0.0)
    cols_h[...], cols_l[...] = halves(jnp.concatenate([lefts, fine_weight(gap), rights], axis=0))
    high, low = halves(jnp.concatenate([lefts[col_count - H :], rights[:H]], axis=0))
    side3[...] = jnp.concatenate([high, high, low], axis=0)
    shape = (row_count, row_count)
    rows_h[...], rows_l[...] = halves(fine_weight(iota(shape, 0) - iota(shape, 1)))
    for load in loads[:4]:
        load.wait()
    shots = doses_ref.shape[-1]
    share = kinds / shots
    live = (iota((1, shots), 1) < count_ref[...]).astype(jnp.float32)
    chosen = (type_ref[0] == iota((kinds, shots), 0)).astype(jnp.float32)
    coef0 = share * jnp.broadcast_to(
        jnp.sum(chosen * (live * doses_ref[0]), axis=1, keepdims=True), (kinds, col_count)
    )
    for kind in range(kinds):
        wf[kind] = w_ref[kind].astype(jnp.float32)
    first = dose_map(coef0)

    pl.semaphore_wait(barrier, len(peers))
    send(0, first)
    loads[4].wait()
    send(COTANGENT, cot_ref[...])

    shape = (row_count, 2 * H)
    spot = iota(shape, 1)
    above = jnp.where(ia > 0, fine_weight(iota(shape, 0) - (spot - H)), 0.0)
    below = jnp.where(ia < na - 1, fine_weight(iota(shape, 0) - (spot - H + row_count)), 0.0)
    high, low = halves(jnp.where(spot < H, above, below))
    edge3[...] = jnp.concatenate([high, high, low], axis=1)
    shape = (groups * coarse_rows, na * packed)
    target = ia * coarse_rows + iota(shape, 0) % coarse_rows
    high, low = halves(back_weight(target - (iota(shape, 1) * groups + iota(shape, 0) // coarse_rows)))
    along3[...] = jnp.concatenate([high, high, low], axis=1)
    shape = (nc * LANES, col_count)
    source = iota(shape, 0) // LANES * coarse_cols + iota(shape, 0) % coarse_cols
    across_h[...], across_l[...] = halves(
        back_weight(source - (ic * coarse_cols + iota(shape, 1) // BLOCK), back_ratio)
    )
    totals = weighted(None)

    inside(0)
    ratio0 = weighted(finish(0)) / totals
    coef1 = coef0 / ratio0
    send(1, dose_map(coef1))

    inside(1)
    inside(COTANGENT)
    grad2 = weighted(finish(COTANGENT))
    ratio1 = weighted(finish(1)) / totals
    coef2 = coef1 / ratio1
    grad_ratio1 = -grad2 * coef2 / ratio1
    send(2, dose_map(grad_ratio1 / totals))
    send(EXPOSURE, dose_map(coef2))

    inside(2)
    grad1 = grad2 / ratio1 + weighted(finish(2))
    grad_ratio0 = -grad1 * coef1 / ratio0
    send(3, dose_map(grad_ratio0 / totals))

    inside(3)
    inside(EXPOSURE)
    out_ref[...] = finish(EXPOSURE)
    grad0 = grad1 / ratio0 + weighted(finish(3))
    grad_ref[0] = live * share * jnp.sum(chosen * grad0[:, 0:1], axis=0, keepdims=True)

    for t in range(JOBS):
        ca, strip, side, ga, halo_rows, halo_cols = jobs[t]
        wait_for(ga.at[: na * nc - 1], send_sems.at[t, 0])
        wait_for(halo_rows, send_sems.at[t, 1])
        wait_for(halo_cols, send_sems.at[t, 2])


def shards(na, nc, doses, shot_type, shot_count, dose_weights, cotangent):
    kinds, rows, cols = dose_weights.shape
    f32, bf16 = jnp.float32, jnp.bfloat16
    coarse_rows = rows // BLOCK
    packed = coarse_rows * (cols // BLOCK) // LANES

    def pair(*shape):
        return [pltpu.VMEM(shape, bf16), pltpu.VMEM(shape, bf16)]

    scratch = [pltpu.VMEM((kinds, rows, cols), f32)] + [pltpu.VMEM((JOBS, rows, cols), f32)] * 2
    scratch += pair(3 * cols, cols) + [pltpu.VMEM((6 * H, cols), bf16)]
    scratch += pair(rows, rows) + [pltpu.VMEM((rows, 6 * H), bf16)]
    groups = coarse_rows // packed
    scratch += [pltpu.VMEM((groups * coarse_rows, 3 * na * packed), bf16)] + pair(nc * LANES, cols)
    for _ in range(JOBS):
        scratch += [
            pltpu.VMEM((packed, LANES), f32),
            pltpu.VMEM((2, H, cols), f32),
            pltpu.VMEM((2, H, rows), f32),
            pltpu.VMEM((na * nc, packed, LANES), f32),
            pltpu.VMEM((3, 2, H, cols), f32),
            pltpu.VMEM((2, H, rows), f32),
        ]
    scratch += [pltpu.SemaphoreType.DMA((JOBS, 3)), pltpu.SemaphoreType.DMA((JOBS, 3))]
    operands = (doses, shot_type, shot_count, dose_weights, cotangent)
    scratch += [pltpu.SemaphoreType.DMA((len(operands),))]
    scratch += [pltpu.VMEM(operand.shape, operand.dtype) for operand in operands]
    return pl.pallas_call(
        functools.partial(kernel, na, nc),
        out_shape=(
            jax.ShapeDtypeStruct(cotangent.shape, f32),
            jax.ShapeDtypeStruct(doses.shape, f32),
        ),
        in_specs=[pl.BlockSpec(memory_space=pltpu.HBM)] * 5,
        out_specs=(pl.BlockSpec(memory_space=pltpu.VMEM),) * 2,
        scratch_shapes=scratch,
        compiler_params=pltpu.CompilerParams(
            collective_id=0, has_side_effects=True, vmem_limit_bytes=64 * 1024 * 1024
        ),
    )(*operands)


def solution(mesh):
    in_specs = (
        P(("groups", "along"), "across", None),
        P(("groups", "along"), "across", None),
        P(("groups", "along"), "across"),
        P(None, ("groups", "along"), "across"),
        P(("groups", "along"), "across"),
    )
    out_specs = (P(("groups", "along"), "across"), P(("groups", "along"), "across", None))
    run = functools.partial(shards, mesh.shape["along"], mesh.shape["across"])
    return jax.shard_map(run, mesh=mesh, in_specs=in_specs, out_specs=out_specs, check_vma=False)
```

```python
import functools
import math

import jax
import jax.numpy as jnp
import numpy as np
from jax import lax
from jax.experimental import pallas as pl
from jax.experimental.pallas import tpu as pltpu
from jax.sharding import PartitionSpec as P

H = 16
LANES = 128
BLOCK = 8
sigma_fine = 3.75
sigma_back = 156.25
back_ratio = 0.7
JOBS = 6
COTANGENT, EXPOSURE = 4, 5
reach = np.arange(-H, H + 1).astype(np.float64)
fine_norm = float(np.sum(np.exp(-reach * reach / (2.0 * sigma_fine * sigma_fine))))


def fine_weight(distance):
    d = distance.astype(jnp.float32)
    return jnp.where(
        jnp.abs(distance) <= H, jnp.exp(-d * d / (2.0 * sigma_fine * sigma_fine)) / fine_norm, 0.0
    )


def back_weight(distance, factor=1.0):
    d = distance.astype(jnp.float32)
    return jnp.exp(-d * d / (2.0 * sigma_back * sigma_back)) * (
        factor / (math.sqrt(2.0 * math.pi) * sigma_back)
    )


def iota(shape, dim):
    return lax.broadcasted_iota(jnp.int32, shape, dim)


def halves(value):
    high = value.astype(jnp.bfloat16)
    return high, (value - high.astype(jnp.float32)).astype(jnp.bfloat16)


def mm(a, b):
    return jnp.dot(a, b, preferred_element_type=jnp.float32)


def dot3(a, b):
    return mm(a[0], b[0]) + (mm(a[0], b[1]) + mm(a[1], b[0]))


def kernel(na, nc, *refs):
    *sources, out_ref, grad_ref = refs[:7]
    (
        wf, fld, fine, cols_h, cols_l, side3, rows_h, rows_l, edge3, along3, across_h, across_l,
    ) = refs[7:19]
    jobs = [refs[19 + 6 * t : 25 + 6 * t] for t in range(JOBS)]
    send_sems, recv_sems, load_sems, *held = refs[19 + 6 * JOBS :]
    doses_ref, type_ref, count_ref, w_ref, cot_ref = held
    loads = [
        pltpu.make_async_copy(source, target, load_sems.at[n])
        for n, (source, target) in enumerate(zip(sources, held))
    ]
    for n in (3, 0, 1, 2, 4):
        loads[n].start()
    kinds, row_count, col_count = w_ref.shape
    coarse_rows = row_count // BLOCK
    coarse_cols = col_count // BLOCK
    groups = LANES // coarse_cols
    packed = coarse_rows // groups
    ia = lax.axis_index("along")
    ic = lax.axis_index("across")
    along_at = [lax.rem(ia + o, na) for o in range(na)]
    across_at = [lax.rem(ic + o, nc) for o in range(nc)]
    up, down = along_at[na - 1], along_at[1]
    left, right = across_at[nc - 1], across_at[1]
    offsets = sorted(range(na), key=lambda o: -min(o, na - o))
    peers = [
        {"along": along_at[oa], "across": across_at[oc]}
        for oa in offsets
        for oc in range(nc)
        if oa or oc
    ]

    has_up, has_down = ia > 0, ia < na - 1

    for tb, edge in ((0, ia == 0), (1, ia == na - 1)):

        @pl.when(edge)
        def _():
            for t in range(JOBS):
                jobs[t][4][tb] = jnp.zeros(jobs[t][4].shape[1:], jnp.float32)

    barrier = pltpu.get_barrier_semaphore()
    for device in peers:
        pl.semaphore_signal(barrier, inc=1, device_id=device, device_id_type=pl.DeviceIdType.MESH)

    lane_group = iota((groups, LANES), 1) // coarse_cols
    pool = jnp.where(
        iota((col_count, LANES), 0) // BLOCK == iota((col_count, LANES), 1) % coarse_cols,
        1.0 / (BLOCK * BLOCK),
        0.0,
    ).astype(jnp.bfloat16)

    def dose_map(coef):
        total = coef[0:1] * wf[0]
        for kind in range(1, kinds):
            total = total + coef[kind : kind + 1] * wf[kind]
        return total

    def weighted(field):
        sums = []
        for kind in range(kinds):
            value = wf[kind] if field is None else wf[kind] * field
            part = value.reshape(row_count // 8, 8, col_count).sum(axis=0)
            sums.append(jnp.sum(part, axis=0, keepdims=True))
        return jnp.broadcast_to(
            jnp.sum(jnp.concatenate(sums, axis=0), axis=1, keepdims=True), (kinds, col_count)
        )

    def remote(src, dst, t, which, device):
        pltpu.make_async_remote_copy(
            src_ref=src,
            dst_ref=dst,
            send_sem=send_sems.at[t, which],
            recv_sem=recv_sems.at[t, which],
            device_id=device,
            device_id_type=pl.DeviceIdType.MESH,
        ).start()

    def wait_for(ref, sem):
        pltpu.make_async_copy(ref, ref, sem).wait()

    mine = ia * nc + ic

    def send(t, field):
        ca, strip, side, ga, halo_rows, halo_cols = jobs[t]
        high, low = halves(field)
        pooled = mm(high, pool) + mm(low, pool)
        for r in range(packed):
            total = None
            for g in range(groups):
                start = (r * groups + g) * BLOCK
                term = jnp.where(lane_group == g, pooled[start : start + BLOCK], 0.0)
                total = term if total is None else total + term
            ca[r : r + 1] = jnp.sum(total, axis=0, keepdims=True)
        for device in peers:
            remote(ca, ga.at[mine], t, 0, device)
        pltpu.make_async_copy(ca, ga.at[mine], recv_sems.at[t, 0]).start()
        strip[0] = field[:H]
        strip[1] = field[row_count - H :]
        turned = field.T
        side[0] = turned[:H]
        side[1] = turned[col_count - H :]
        for tb, a, some in ((0, up, has_up), (1, down, has_down)):

            @pl.when(some)
            def _():
                for slot, c in ((1, ic), (2, left), (0, right)):
                    device = {"along": a, "across": c}
                    remote(strip.at[tb], halo_rows.at[1 - tb, slot], t, 2 - tb, device)

        remote(side.at[0], halo_cols.at[1], t, 3, {"along": ia, "across": left})
        remote(side.at[1], halo_cols.at[0], t, 3, {"along": ia, "across": right})
        fld[t] = field

    def inside(t):
        centre = (cols_h[col_count : 2 * col_count], cols_l[col_count : 2 * col_count])
        middle = dot3(halves(fld[t]), centre)
        fine[t] = dot3((rows_h[...], rows_l[...]), halves(middle))

    def finish(t):
        ca, strip, side, ga, halo_rows, halo_cols = jobs[t]
        for tb, some in ((0, has_up), (1, has_down)):

            @pl.when(some)
            def _():
                wait_for(halo_rows.at[tb], recv_sems.at[t, 1 + tb])

        wait_for(halo_cols, recv_sems.at[t, 3])
        high, low = halves(jnp.concatenate([halo_cols[0], halo_cols[1]], axis=0).T)
        beside = mm(jnp.concatenate([high, low, high], axis=1), side3[...])
        outer = jnp.concatenate(
            [jnp.concatenate([halo_rows[0, s], halo_rows[1, s]], axis=0) for s in range(3)], axis=1
        )
        high, low = halves(dot3(halves(outer), (cols_h[...], cols_l[...])))
        edges = mm(edge3[...], jnp.concatenate([high, low, high], axis=0))
        result = fine[t] + (dot3((rows_h[...], rows_l[...]), halves(beside)) + edges)

        wait_for(ga, recv_sems.at[t, 0])
        theirs = jnp.concatenate(
            [
                jnp.concatenate([ga[a * nc + c] for a in range(na)], axis=0)
                for c in range(nc)
            ],
            axis=1,
        )
        high, low = halves(theirs)
        every = mm(along3[...], jnp.concatenate([high, low, high], axis=0))
        picked = None
        group = iota((coarse_rows, nc * LANES), 1) % LANES // coarse_cols
        for g in range(groups):
            term = jnp.where(group == g, every[g * coarse_rows : (g + 1) * coarse_rows], 0.0)
            picked = term if picked is None else picked + term
        back = dot3(halves(picked), (across_h[...], across_l[...]))
        return result + jnp.concatenate(
            [jnp.broadcast_to(back[p : p + 1], (BLOCK, col_count)) for p in range(coarse_rows)],
            axis=0,
        )

    shape = (col_count, col_count)
    gap = iota(shape, 1) - iota(shape, 0)
    lefts = jnp.where(ic > 0, fine_weight(gap + col_count), 0.0)
    rights = jnp.where(ic < nc - 1, fine_weight(gap - col_count), 0.0)
    cols_h[...], cols_l[...] = halves(jnp.concatenate([lefts, fine_weight(gap), rights], axis=0))
    high, low = halves(jnp.concatenate([lefts[col_count - H :], rights[:H]], axis=0))
    side3[...] = jnp.concatenate([high, high, low], axis=0)
    shape = (row_count, row_count)
    rows_h[...], rows_l[...] = halves(fine_weight(iota(shape, 0) - iota(shape, 1)))
    for load in loads[:4]:
        load.wait()
    shots = doses_ref.shape[-1]
    share = kinds / shots
    live = (iota((1, shots), 1) < count_ref[...]).astype(jnp.float32)
    chosen = (type_ref[0] == iota((kinds, shots), 0)).astype(jnp.float32)
    coef0 = share * jnp.broadcast_to(
        jnp.sum(chosen * (live * doses_ref[0]), axis=1, keepdims=True), (kinds, col_count)
    )
    for kind in range(kinds):
        wf[kind] = w_ref[kind].astype(jnp.float32)
    first = dose_map(coef0)

    pl.semaphore_wait(barrier, len(peers))
    send(0, first)
    loads[4].wait()
    send(COTANGENT, cot_ref[...])

    shape = (row_count, 2 * H)
    spot = iota(shape, 1)
    above = jnp.where(ia > 0, fine_weight(iota(shape, 0) - (spot - H)), 0.0)
    below = jnp.where(ia < na - 1, fine_weight(iota(shape, 0) - (spot - H + row_count)), 0.0)
    high, low = halves(jnp.where(spot < H, above, below))
    edge3[...] = jnp.concatenate([high, high, low], axis=1)
    shape = (groups * coarse_rows, na * packed)
    target = ia * coarse_rows + iota(shape, 0) % coarse_rows
    high, low = halves(back_weight(target - (iota(shape, 1) * groups + iota(shape, 0) // coarse_rows)))
    along3[...] = jnp.concatenate([high, high, low], axis=1)
    shape = (nc * LANES, col_count)
    source = iota(shape, 0) // LANES * coarse_cols + iota(shape, 0) % coarse_cols
    across_h[...], across_l[...] = halves(
        back_weight(source - (ic * coarse_cols + iota(shape, 1) // BLOCK), back_ratio)
    )
    totals = weighted(None)

    inside(0)
    ratio0 = weighted(finish(0)) / totals
    coef1 = coef0 / ratio0
    send(1, dose_map(coef1))

    inside(1)
    inside(COTANGENT)
    grad2 = weighted(finish(COTANGENT))
    ratio1 = weighted(finish(1)) / totals
    coef2 = coef1 / ratio1
    grad_ratio1 = -grad2 * coef2 / ratio1
    send(2, dose_map(grad_ratio1 / totals))
    send(EXPOSURE, dose_map(coef2))

    inside(2)
    grad1 = grad2 / ratio1 + weighted(finish(2))
    grad_ratio0 = -grad1 * coef1 / ratio0
    send(3, dose_map(grad_ratio0 / totals))

    inside(3)
    inside(EXPOSURE)
    out_ref[...] = finish(EXPOSURE)
    grad0 = grad1 / ratio0 + weighted(finish(3))
    grad_ref[0] = live * share * jnp.sum(chosen * grad0[:, 0:1], axis=0, keepdims=True)

    for t in range(JOBS):
        ca, strip, side, ga, halo_rows, halo_cols = jobs[t]
        wait_for(ga.at[: na * nc - 1], send_sems.at[t, 0])
        for tb, some in ((0, has_down), (1, has_up)):

            @pl.when(some)
            def _():
                wait_for(halo_rows.at[tb], send_sems.at[t, 1 + tb])

        wait_for(halo_cols, send_sems.at[t, 3])


def shards(na, nc, doses, shot_type, shot_count, dose_weights, cotangent):
    kinds, rows, cols = dose_weights.shape
    f32, bf16 = jnp.float32, jnp.bfloat16
    coarse_rows = rows // BLOCK
    packed = coarse_rows * (cols // BLOCK) // LANES

    def pair(*shape):
        return [pltpu.VMEM(shape, bf16), pltpu.VMEM(shape, bf16)]

    scratch = [pltpu.VMEM((kinds, rows, cols), f32)] + [pltpu.VMEM((JOBS, rows, cols), f32)] * 2
    scratch += pair(3 * cols, cols) + [pltpu.VMEM((6 * H, cols), bf16)]
    scratch += pair(rows, rows) + [pltpu.VMEM((rows, 6 * H), bf16)]
    groups = coarse_rows // packed
    scratch += [pltpu.VMEM((groups * coarse_rows, 3 * na * packed), bf16)] + pair(nc * LANES, cols)
    for _ in range(JOBS):
        scratch += [
            pltpu.VMEM((packed, LANES), f32),
            pltpu.VMEM((2, H, cols), f32),
            pltpu.VMEM((2, H, rows), f32),
            pltpu.VMEM((na * nc, packed, LANES), f32),
            pltpu.VMEM((2, 3, H, cols), f32),
            pltpu.VMEM((2, H, rows), f32),
        ]
    scratch += [pltpu.SemaphoreType.DMA((JOBS, 4)), pltpu.SemaphoreType.DMA((JOBS, 4))]
    operands = (doses, shot_type, shot_count, dose_weights, cotangent)
    scratch += [pltpu.SemaphoreType.DMA((len(operands),))]
    scratch += [pltpu.VMEM(operand.shape, operand.dtype) for operand in operands]
    return pl.pallas_call(
        functools.partial(kernel, na, nc),
        out_shape=(
            jax.ShapeDtypeStruct(cotangent.shape, f32),
            jax.ShapeDtypeStruct(doses.shape, f32),
        ),
        in_specs=[pl.BlockSpec(memory_space=pltpu.HBM)] * 5,
        out_specs=(pl.BlockSpec(memory_space=pltpu.VMEM),) * 2,
        scratch_shapes=scratch,
        compiler_params=pltpu.CompilerParams(
            collective_id=0, has_side_effects=True, vmem_limit_bytes=64 * 1024 * 1024
        ),
    )(*operands)


def solution(mesh):
    in_specs = (
        P(("groups", "along"), "across", None),
        P(("groups", "along"), "across", None),
        P(("groups", "along"), "across"),
        P(None, ("groups", "along"), "across"),
        P(("groups", "along"), "across"),
    )
    out_specs = (P(("groups", "along"), "across"), P(("groups", "along"), "across", None))
    run = functools.partial(shards, mesh.shape["along"], mesh.shape["across"])
    return jax.shard_map(run, mesh=mesh, in_specs=in_specs, out_specs=out_specs, check_vma=False)
```

```python
import functools
import math

import jax
import jax.numpy as jnp
import numpy as np
from jax import lax
from jax.experimental import pallas as pl
from jax.experimental.pallas import tpu as pltpu
from jax.sharding import PartitionSpec as P

H = 16
LANES = 128
BLOCK = 8
sigma_fine = 3.75
sigma_back = 156.25
back_ratio = 0.7
JOBS = 6
COTANGENT, EXPOSURE = 4, 5
reach = np.arange(-H, H + 1).astype(np.float64)
fine_norm = float(np.sum(np.exp(-reach * reach / (2.0 * sigma_fine * sigma_fine))))


def fine_weight(distance):
    d = distance.astype(jnp.float32)
    return jnp.where(
        jnp.abs(distance) <= H, jnp.exp(-d * d / (2.0 * sigma_fine * sigma_fine)) / fine_norm, 0.0
    )


def back_weight(distance, factor=1.0):
    d = distance.astype(jnp.float32)
    return jnp.exp(-d * d / (2.0 * sigma_back * sigma_back)) * (
        factor / (math.sqrt(2.0 * math.pi) * sigma_back)
    )


def iota(shape, dim):
    return lax.broadcasted_iota(jnp.int32, shape, dim)


def halves(value):
    high = value.astype(jnp.bfloat16)
    return high, (value - high.astype(jnp.float32)).astype(jnp.bfloat16)


def mm(a, b):
    return jnp.dot(a, b, preferred_element_type=jnp.float32)


def dot3(a, b):
    return mm(a[0], b[0]) + (mm(a[0], b[1]) + mm(a[1], b[0]))


def kernel(na, nc, *refs):
    *sources, out_ref, grad_ref = refs[:7]
    (
        wf, fld, fine, cols_h, cols_l, side3, rows_h, rows_l, edge3, along3, across_h, across_l,
    ) = refs[7:19]
    jobs = [refs[19 + 6 * t : 25 + 6 * t] for t in range(JOBS)]
    send_sems, recv_sems, load_sems, *held = refs[19 + 6 * JOBS :]
    doses_ref, type_ref, count_ref, w_ref, cot_ref = held
    loads = [
        pltpu.make_async_copy(source, target, load_sems.at[n])
        for n, (source, target) in enumerate(zip(sources, held))
    ]
    for n in (3, 0, 1, 2, 4):
        loads[n].start()
    kinds, row_count, col_count = w_ref.shape
    coarse_rows = row_count // BLOCK
    coarse_cols = col_count // BLOCK
    groups = LANES // coarse_cols
    packed = coarse_rows // groups
    ia = lax.axis_index("along")
    ic = lax.axis_index("across")
    along_at = [lax.rem(ia + o, na) for o in range(na)]
    across_at = [lax.rem(ic + o, nc) for o in range(nc)]
    up, down = along_at[na - 1], along_at[1]
    left, right = across_at[nc - 1], across_at[1]
    offsets = sorted(range(na), key=lambda o: -min(o, na - o))
    peers = [
        {"along": along_at[oa], "across": across_at[oc]}
        for oa in offsets
        for oc in range(nc)
        if oa or oc
    ]

    has_up, has_down = ia > 0, ia < na - 1

    for tb, edge in ((0, ia == 0), (1, ia == na - 1)):

        @pl.when(edge)
        def _():
            for t in range(JOBS):
                jobs[t][4][tb] = jnp.zeros(jobs[t][4].shape[1:], jnp.float32)

    barrier = pltpu.get_barrier_semaphore()
    for device in peers:
        pl.semaphore_signal(barrier, inc=1, device_id=device, device_id_type=pl.DeviceIdType.MESH)

    lane_group = iota((groups, LANES), 1) // coarse_cols
    pool = jnp.where(
        iota((col_count, LANES), 0) // BLOCK == iota((col_count, LANES), 1) % coarse_cols,
        1.0 / (BLOCK * BLOCK),
        0.0,
    ).astype(jnp.bfloat16)

    def dose_map(coef):
        total = coef[0:1] * wf[0]
        for kind in range(1, kinds):
            total = total + coef[kind : kind + 1] * wf[kind]
        return total

    def weighted(field):
        sums = []
        for kind in range(kinds):
            value = wf[kind] if field is None else wf[kind] * field
            part = value.reshape(row_count // 8, 8, col_count).sum(axis=0)
            sums.append(jnp.sum(part, axis=0, keepdims=True))
        return jnp.broadcast_to(
            jnp.sum(jnp.concatenate(sums, axis=0), axis=1, keepdims=True), (kinds, col_count)
        )

    def remote(src, dst, t, which, device):
        pltpu.make_async_remote_copy(
            src_ref=src,
            dst_ref=dst,
            send_sem=send_sems.at[t, which],
            recv_sem=recv_sems.at[t, which],
            device_id=device,
            device_id_type=pl.DeviceIdType.MESH,
        ).start()

    def wait_for(ref, sem):
        pltpu.make_async_copy(ref, ref, sem).wait()

    mine = ia * nc + ic

    def send(t, field):
        ca, strip, side, ga, halo_rows, halo_cols = jobs[t]
        high, low = halves(field)
        pooled = mm(high, pool) + mm(low, pool)
        for r in range(packed):
            total = None
            for g in range(groups):
                start = (r * groups + g) * BLOCK
                term = jnp.where(lane_group == g, pooled[start : start + BLOCK], 0.0)
                total = term if total is None else total + term
            ca[r : r + 1] = jnp.sum(total, axis=0, keepdims=True)
        for device in peers:
            remote(ca, ga.at[mine], t, 0, device)
        pltpu.make_async_copy(ca, ga.at[mine], recv_sems.at[t, 0]).start()
        strip[0] = field[:H]
        strip[1] = field[row_count - H :]
        turned = field.T
        side[0] = turned[:H]
        side[1] = turned[col_count - H :]
        for tb, a, some in ((0, up, has_up), (1, down, has_down)):

            @pl.when(some)
            def _():
                for slot, c in ((1, ic), (2, left), (0, right)):
                    device = {"along": a, "across": c}
                    remote(strip.at[tb], halo_rows.at[1 - tb, slot], t, 2 - tb, device)

        remote(side.at[0], halo_cols.at[1], t, 3, {"along": ia, "across": left})
        remote(side.at[1], halo_cols.at[0], t, 3, {"along": ia, "across": right})
        fld[t] = field

    def inside(t):
        centre = (cols_h[col_count : 2 * col_count], cols_l[col_count : 2 * col_count])
        middle = dot3(halves(fld[t]), centre)
        fine[t] = dot3((rows_h[...], rows_l[...]), halves(middle))

    def finish(t):
        ca, strip, side, ga, halo_rows, halo_cols = jobs[t]
        for tb, some in ((0, has_up), (1, has_down)):

            @pl.when(some)
            def _():
                wait_for(halo_rows.at[tb], recv_sems.at[t, 1 + tb])

        wait_for(halo_cols, recv_sems.at[t, 3])
        high, low = halves(jnp.concatenate([halo_cols[0], halo_cols[1]], axis=0).T)
        beside = mm(jnp.concatenate([high, low, high], axis=1), side3[...])
        outer = jnp.concatenate(
            [jnp.concatenate([halo_rows[0, s], halo_rows[1, s]], axis=0) for s in range(3)], axis=1
        )
        high, low = halves(dot3(halves(outer), (cols_h[...], cols_l[...])))
        edges = mm(edge3[...], jnp.concatenate([high, low, high], axis=0))
        result = fine[t] + (dot3((rows_h[...], rows_l[...]), halves(beside)) + edges)

        wait_for(ga, recv_sems.at[t, 0])
        theirs = jnp.concatenate(
            [
                jnp.concatenate([ga[a * nc + c] for a in range(na)], axis=0)
                for c in range(nc)
            ],
            axis=1,
        )
        high, low = halves(theirs)
        every = mm(along3[...], jnp.concatenate([high, low, high], axis=0))
        picked = None
        group = iota((coarse_rows, nc * LANES), 1) % LANES // coarse_cols
        for g in range(groups):
            term = jnp.where(group == g, every[g * coarse_rows : (g + 1) * coarse_rows], 0.0)
            picked = term if picked is None else picked + term
        back = dot3(halves(picked), (across_h[...], across_l[...]))
        return result + jnp.concatenate(
            [jnp.broadcast_to(back[p : p + 1], (BLOCK, col_count)) for p in range(coarse_rows)],
            axis=0,
        )

    shape = (col_count, col_count)
    gap = iota(shape, 1) - iota(shape, 0)
    lefts = jnp.where(ic > 0, fine_weight(gap + col_count), 0.0)
    rights = jnp.where(ic < nc - 1, fine_weight(gap - col_count), 0.0)
    cols_h[...], cols_l[...] = halves(jnp.concatenate([lefts, fine_weight(gap), rights], axis=0))
    high, low = halves(jnp.concatenate([lefts[col_count - H :], rights[:H]], axis=0))
    side3[...] = jnp.concatenate([high, high, low], axis=0)
    shape = (row_count, row_count)
    rows_h[...], rows_l[...] = halves(fine_weight(iota(shape, 0) - iota(shape, 1)))
    for load in loads[:4]:
        load.wait()
    shots = doses_ref.shape[-1]
    share = kinds / shots
    live = (iota((1, shots), 1) < count_ref[...]).astype(jnp.float32)
    chosen = (type_ref[0] == iota((kinds, shots), 0)).astype(jnp.float32)
    coef0 = share * jnp.broadcast_to(
        jnp.sum(chosen * (live * doses_ref[0]), axis=1, keepdims=True), (kinds, col_count)
    )
    for kind in range(kinds):
        wf[kind] = w_ref[kind].astype(jnp.float32)
    first = dose_map(coef0)

    pl.semaphore_wait(barrier, len(peers))
    send(0, first)
    loads[4].wait()

    shape = (row_count, 2 * H)
    spot = iota(shape, 1)
    above = jnp.where(ia > 0, fine_weight(iota(shape, 0) - (spot - H)), 0.0)
    below = jnp.where(ia < na - 1, fine_weight(iota(shape, 0) - (spot - H + row_count)), 0.0)
    high, low = halves(jnp.where(spot < H, above, below))
    edge3[...] = jnp.concatenate([high, high, low], axis=1)
    shape = (groups * coarse_rows, na * packed)
    target = ia * coarse_rows + iota(shape, 0) % coarse_rows
    high, low = halves(back_weight(target - (iota(shape, 1) * groups + iota(shape, 0) // coarse_rows)))
    along3[...] = jnp.concatenate([high, high, low], axis=1)
    shape = (nc * LANES, col_count)
    source = iota(shape, 0) // LANES * coarse_cols + iota(shape, 0) % coarse_cols
    across_h[...], across_l[...] = halves(
        back_weight(source - (ic * coarse_cols + iota(shape, 1) // BLOCK), back_ratio)
    )
    totals = weighted(None)

    inside(0)
    send(COTANGENT, cot_ref[...])
    ratio0 = weighted(finish(0)) / totals
    coef1 = coef0 / ratio0
    send(1, dose_map(coef1))

    inside(1)
    inside(COTANGENT)
    grad2 = weighted(finish(COTANGENT))
    ratio1 = weighted(finish(1)) / totals
    coef2 = coef1 / ratio1
    grad_ratio1 = -grad2 * coef2 / ratio1
    send(2, dose_map(grad_ratio1 / totals))

    inside(2)
    send(EXPOSURE, dose_map(coef2))
    grad1 = grad2 / ratio1 + weighted(finish(2))
    grad_ratio0 = -grad1 * coef1 / ratio0
    send(3, dose_map(grad_ratio0 / totals))

    inside(3)
    inside(EXPOSURE)
    out_ref[...] = finish(EXPOSURE)
    grad0 = grad1 / ratio0 + weighted(finish(3))
    grad_ref[0] = live * share * jnp.sum(chosen * grad0[:, 0:1], axis=0, keepdims=True)

    for t in range(JOBS):
        ca, strip, side, ga, halo_rows, halo_cols = jobs[t]
        wait_for(ga.at[: na * nc - 1], send_sems.at[t, 0])
        for tb, some in ((0, has_down), (1, has_up)):

            @pl.when(some)
            def _():
                wait_for(halo_rows.at[tb], send_sems.at[t, 1 + tb])

        wait_for(halo_cols, send_sems.at[t, 3])


def shards(na, nc, doses, shot_type, shot_count, dose_weights, cotangent):
    kinds, rows, cols = dose_weights.shape
    f32, bf16 = jnp.float32, jnp.bfloat16
    coarse_rows = rows // BLOCK
    packed = coarse_rows * (cols // BLOCK) // LANES

    def pair(*shape):
        return [pltpu.VMEM(shape, bf16), pltpu.VMEM(shape, bf16)]

    scratch = [pltpu.VMEM((kinds, rows, cols), f32)] + [pltpu.VMEM((JOBS, rows, cols), f32)] * 2
    scratch += pair(3 * cols, cols) + [pltpu.VMEM((6 * H, cols), bf16)]
    scratch += pair(rows, rows) + [pltpu.VMEM((rows, 6 * H), bf16)]
    groups = coarse_rows // packed
    scratch += [pltpu.VMEM((groups * coarse_rows, 3 * na * packed), bf16)] + pair(nc * LANES, cols)
    for _ in range(JOBS):
        scratch += [
            pltpu.VMEM((packed, LANES), f32),
            pltpu.VMEM((2, H, cols), f32),
            pltpu.VMEM((2, H, rows), f32),
            pltpu.VMEM((na * nc, packed, LANES), f32),
            pltpu.VMEM((2, 3, H, cols), f32),
            pltpu.VMEM((2, H, rows), f32),
        ]
    scratch += [pltpu.SemaphoreType.DMA((JOBS, 4)), pltpu.SemaphoreType.DMA((JOBS, 4))]
    operands = (doses, shot_type, shot_count, dose_weights, cotangent)
    scratch += [pltpu.SemaphoreType.DMA((len(operands),))]
    scratch += [pltpu.VMEM(operand.shape, operand.dtype) for operand in operands]
    return pl.pallas_call(
        functools.partial(kernel, na, nc),
        out_shape=(
            jax.ShapeDtypeStruct(cotangent.shape, f32),
            jax.ShapeDtypeStruct(doses.shape, f32),
        ),
        in_specs=[pl.BlockSpec(memory_space=pltpu.HBM)] * 5,
        out_specs=(pl.BlockSpec(memory_space=pltpu.VMEM),) * 2,
        scratch_shapes=scratch,
        compiler_params=pltpu.CompilerParams(
            collective_id=0, has_side_effects=True, vmem_limit_bytes=64 * 1024 * 1024
        ),
    )(*operands)


def solution(mesh):
    in_specs = (
        P(("groups", "along"), "across", None),
        P(("groups", "along"), "across", None),
        P(("groups", "along"), "across"),
        P(None, ("groups", "along"), "across"),
        P(("groups", "along"), "across"),
    )
    out_specs = (P(("groups", "along"), "across"), P(("groups", "along"), "across", None))
    run = functools.partial(shards, mesh.shape["along"], mesh.shape["across"])
    return jax.shard_map(run, mesh=mesh, in_specs=in_specs, out_specs=out_specs, check_vma=False)
```
